512 devices in a mesh: replica: 8 (over z), pipe: 4 (over x), tensor: 16 (over y, core).
Axes of the slice: x: 4, y: 8, z: 8, core: 2. Of those that a mesh axis runs over, the one named last changes fastest.
Arguments:
- queries: bfloat16 [1024, 8192], P('replica', ('pipe', 'tensor')), parts along dimension 0, may hold values from -128 to 128, as said below
- cache_keys: bfloat16 [32, 4096, 1024], P('replica', 'tensor', 'pipe'), parts along dimension 0, may hold values from -4 to 4
- cache_values: bfloat16 [32, 4096, 1024], P('replica', 'tensor', 'pipe'), parts along dimension 0, may hold values from -6 to 6
- prefix_lengths: int32 [32], P('replica'), parts along dimension 0, may hold values from 2048 to 4064
- residual_in: bfloat16 [1024, 8192], P('replica', ('pipe', 'tensor')), parts along dimension 0, may hold values from -64 to 64
- out_weight: bfloat16 [8192, 4, 2048], P('pipe', None, 'tensor'), may hold values from -0.0625 to 0.0625
- norm_gain: float32 [8192], P(('pipe', 'tensor')), may hold values from 0.1 to 1.9
Outputs:
- residual_out: bfloat16 [1024, 8192], P('replica', ('pipe', 'tensor')), parts along dimension 0
- normed: bfloat16 [1024, 8192], P('replica', ('pipe', 'tensor')), parts along dimension 0
The draws below stay inside these ranges and needn't reach their ends.
There are 8 independent parts, one for each index of `replica`. The reference program is written for one: setup_inputs(seed, part) draws one part's arguments, and reference() takes and returns one part's arrays. A program takes and returns all parts, laid end to end along the dimension named above; an argument that names none is the same for every part. Nothing has to cross between parts.
Inputs may be any that keep to these rules, and one draw needn't show every extreme that they name: `queries`: entries of the query rows; some rows may be much longer than others. The span's own keys and values already stand in the cache, in slots prefix_lengths[r] to prefix_lengths[r] + 31; later slots hold unused entries.
All inputs are finite; a program needn't handle non-finite values.
Results may differ from the reference program's by a relative error of at most 0.018.
Values may be sent and summed in bfloat16 or wider, within the bound.
No kernel may reach another device: no remote copies, remote signals or barrier semaphores. Data moves between devices by JAX's collectives and lax.ppermute only.
A program may use at most 64 MiB of HBM per device.

```python
import math
import jax
import jax.numpy as jnp
from jax import lax

D = 8192
HEADS = 64
KV_HEADS = 8
HD = 128
C = 32
L = 4096
R = 4
N_PIPE = 4


def draw_queries(key, part):
    drawn = 2.5 * jnp.clip(jax.random.normal(jax.random.fold_in(key, 1), (R, C, HEADS, HD), jnp.float32), -6.0, 6.0)
    return drawn.reshape(R * C, HEADS * HD).astype(jnp.bfloat16)


def draw_cache_keys(key, part):
    drawn = jnp.clip(jax.random.normal(jax.random.fold_in(key, 2), (R, L, KV_HEADS, HD), jnp.float32), -4.0, 4.0)
    return drawn.reshape(R, L, KV_HEADS * HD).astype(jnp.bfloat16)


def draw_residual_in(key, part):
    row_scale = 0.03 * jnp.exp(jax.random.uniform(jax.random.fold_in(key, 3), (R * C, 1), jnp.float32, 0.0, math.log(10.0)))
    column_trend = jnp.sqrt(1.0 + 2.0 * jnp.arange(D, dtype=jnp.float32) / max(D - 1, 1))[None, :]
    column_scale = jnp.exp(jax.random.uniform(jax.random.fold_in(key, 4), (1, D), jnp.float32, 0.0, math.log(10.0))) * column_trend
    noise = jnp.clip(jax.random.normal(jax.random.fold_in(key, 6), (R * C, D), jnp.float32), -4.0, 4.0)
    drawn = noise * row_scale * column_scale
    return drawn.astype(jnp.bfloat16)


def touch_ends(entries, own_key, low, high):
    place = [jax.random.randint(jax.random.fold_in(own_key, axis), (), 0, length) for axis, length in enumerate(entries.shape)]
    widest = entries.shape.index(max(entries.shape))
    neighbour = place[:widest] + [(place[widest] + 1) % entries.shape[widest]] + place[widest + 1:]
    return entries.at[tuple(place)].set(low).at[tuple(neighbour)].set(high)


def steps_of(stream_key, dims, split, low, top_value):
    level, own = 1.0, jax.random.fold_in(stream_key, 6)
    for axis_at, blocks in split:
        steps = jnp.exp(jax.random.uniform(jax.random.fold_in(own, axis_at), (blocks,), jnp.float32, low / len(split), top_value / len(split)))
        level = level * jnp.repeat(steps, dims[axis_at] // blocks).reshape([-1 if axis == axis_at else 1 for axis in range(len(dims))])
    return level


def centred(own_key, extent, deviation, most, shards=(), kind=jnp.bfloat16):
    values = deviation * jax.random.normal(own_key, extent, jnp.float32)
    if shards:
        values = values * steps_of(own_key, extent, shards, -0.22, 0.18)
    return jnp.clip(values, -most, most).astype(kind)


def setup_inputs(seed: int = 0, part: int = 0) -> dict:
    streams_of = jax.random.split(jax.random.key(seed), 8)
    part_splits = jax.random.split(jax.random.fold_in(streams_of[7], part), 8)
    return {
        "queries": draw_queries(jax.random.fold_in(jax.random.fold_in(streams_of[7], part), 71), part),
        "cache_keys": draw_cache_keys(jax.random.fold_in(jax.random.fold_in(streams_of[7], part), 71), part),
        "cache_values": centred(part_splits[2], (R, L, KV_HEADS * HD), 1.0, 6.0, ((1, 16), (2, 4))),
        "prefix_lengths": touch_ends(jax.random.randint(part_splits[3], (R,), L // 2, L - C + 1), jax.random.fold_in(part_splits[3], 1), L // 2, L - C).astype(jnp.int32),
        "residual_in": draw_residual_in(jax.random.fold_in(jax.random.fold_in(streams_of[7], part), 71), part),
        "out_weight": centred(streams_of[5], (HEADS * HD, N_PIPE, D // N_PIPE), (HEADS * HD) ** -0.5, 0.0625, ((0, 4), (2, 16))),
        "norm_gain": jnp.clip(1.0 + 0.18 * jax.random.normal(streams_of[6], (D,), jnp.float32), 0.1, 1.9),
    }


masked_value = -1e+30
epsilon = 1e-05

def attend_request(packed):
    request_queries, request_keys, request_values, prefix = packed
    group_size = HEADS // KV_HEADS
    queries_here = request_queries.reshape(C, KV_HEADS, group_size, HD).astype(jnp.float32)
    keys_here = request_keys.reshape(L, KV_HEADS, HD).astype(jnp.float32)
    values_here = request_values.reshape(L, KV_HEADS, HD).astype(jnp.float32)
    scores = jnp.einsum('cghd,jgd->cghj', queries_here, keys_here) * (1.0 / math.sqrt(HD))
    limits = prefix + jnp.arange(C, dtype=jnp.int32)
    visible = jnp.arange(L, dtype=jnp.int32)[None, :] <= limits[:, None]
    visible = visible[:, None, None, :]
    masked = jnp.where(visible, scores, masked_value)
    row_peak = lax.optimization_barrier(jnp.max(masked, axis=-1, keepdims=True))
    weights = jnp.where(visible, jnp.exp(masked - row_peak), 0.0)
    row_total = lax.optimization_barrier(jnp.sum(weights, axis=-1))
    rounded = lax.optimization_barrier(weights.astype(jnp.bfloat16)).astype(jnp.float32)
    summed = jnp.einsum('cghj,jgd->cghd', rounded, values_here)
    return (summed / row_total[..., None]).astype(jnp.bfloat16)

def reference(queries, cache_keys, cache_values, prefix_lengths, residual_in, out_weight, norm_gain):
    per_request = queries.reshape(R, C, HEADS * HD)
    attended = lax.map(attend_request, (per_request, cache_keys, cache_values, prefix_lengths))
    attended = attended.reshape(R * C, HEADS * HD)
    weight_matrix = out_weight.reshape(HEADS * HD, D)
    section_rows = HEADS * HD // N_PIPE
    projected = jnp.zeros((R * C, D), jnp.float32)
    for section_index in range(N_PIPE):
        lower = section_index * section_rows
        section_term = jnp.dot(attended[:, lower:lower + section_rows], weight_matrix[lower:lower + section_rows], preferred_element_type=jnp.float32)
        projected = projected + lax.optimization_barrier(section_term.astype(jnp.bfloat16)).astype(jnp.float32)
    updated = residual_in.astype(jnp.float32) + projected
    squares = lax.optimization_barrier(jnp.sum(updated * updated, axis=1, keepdims=True))
    normed = updated * lax.rsqrt(squares / D + epsilon) * norm_gain.astype(jnp.float32)[None, :]
    return (updated.astype(jnp.bfloat16), normed.astype(jnp.bfloat16))
```

```python
import math

import jax
import jax.numpy as jnp
from jax import lax
from jax.experimental import pallas as pl
from jax.experimental.pallas import tpu as pltpu
from jax.sharding import Mesh
from jax.sharding import PartitionSpec as P

HD = 128
SPAN = 32
MASKED = -1e30
FLOOR = -1e29
EPSILON = 1e-05
STATS = 16

VMEM = pl.BlockSpec(memory_space=pltpu.VMEM)
SMEM = pl.BlockSpec(memory_space=pltpu.SMEM)
F32 = jnp.float32
BF16 = jnp.bfloat16


def call(kernel, out_shape, args, in_specs=None, scratch=(), flops=0, moved=0, name=None):
    return pl.pallas_call(
        kernel,
        out_shape=out_shape,
        in_specs=in_specs or [VMEM] * len(args),
        out_specs=jax.tree.map(lambda _: VMEM, out_shape),
        scratch_shapes=list(scratch),
        compiler_params=pltpu.CompilerParams(vmem_limit_bytes=24 * 2**20),
        cost_estimate=pl.CostEstimate(flops=flops, bytes_accessed=moved, transcendentals=0),
        name=name,
    )(*args)


def attend_kernel(place, prefix, queries, keys, values, others, out):
    core = place[0]
    starts = (place[1], place[2])
    slots = keys.shape[1]
    rows = 8 * SPAN
    ahead = lax.broadcasted_iota(jnp.int32, (slots, rows), 0) - lax.rem(
        lax.broadcasted_iota(jnp.int32, (slots, rows), 1), SPAN
    )
    line = lax.broadcasted_iota(jnp.int32, (STATS, rows), 0)
    scale = math.log2(math.e) / math.sqrt(HD)
    for at in range(2):
        request = 2 * core + at
        for group in range(2):
            columns = pl.ds(group * HD, HD)
            wanted = queries[pl.ds(8 * group, 8), pl.ds(SPAN * at, SPAN), :].reshape(rows, HD)
            pieces = (
                (keys[request, :, columns], values[request, :, columns]),
                (others[0, at, :, columns], others[1, at, :, columns]),
            )
            scores = []
            for (key, _), start in zip(pieces, starts):
                score = lax.dot_general(
                    key, wanted, (((1,), (1,)), ((), ())), preferred_element_type=F32
                )
                scores.append(
                    jnp.where(ahead <= prefix[request] - start, score * scale, MASKED)
                )
            peak = jnp.maximum(*[jnp.max(s, axis=0, keepdims=True) for s in scores])
            peak = jnp.maximum(peak, FLOOR).astype(BF16).astype(F32)
            weights = [jnp.exp2(s - peak) for s in scores]
            total = sum(jnp.sum(w, axis=0, keepdims=True) for w in weights)
            summed = sum(
                lax.dot_general(
                    value, w.astype(BF16), (((0,), (0,)), ((), ())), preferred_element_type=F32
                )
                for (_, value), w in zip(pieces, weights)
            )
            scaled = (summed * jnp.where(total > 0, 1.0 / total, 0.0)).astype(BF16)
            high = total.astype(BF16).astype(F32)
            stats = jnp.where(
                line == 0, peak, jnp.where(line == 1, high, jnp.where(line == 2, total - high, 0.0))
            ).astype(BF16)
            for half in range(2):
                to = 4 * at + 2 * group + half
                lanes = slice(half * HD, (half + 1) * HD)
                out[to, pl.ds(0, HD), :] = scaled[:, lanes]
                out[to, pl.ds(HD, STATS), :] = stats[:, lanes]


def combine_kernel(parts, out):
    count = parts.shape[0]
    stats = [parts[i, pl.ds(HD, STATS), :].astype(F32) for i in range(count)]
    peaks = [s[0:1] for s in stats]
    overall = peaks[0]
    for peak in peaks[1:]:
        overall = jnp.maximum(overall, peak)
    shares = [(s[1:2] + s[2:3]) * jnp.exp2(p - overall) for s, p in zip(stats, peaks)]
    inverse = 1.0 / sum(shares)
    summed = jnp.zeros((HD, HD), F32)
    for i in range(count):
        summed += parts[i, pl.ds(0, HD), :].astype(F32) * (shares[i] * inverse)
    attended = summed.T.astype(BF16)
    for i in range(count):
        out[i] = attended


def project_kernel(attended, weight, out, joined):
    for core in range(2):
        for at in range(2):
            for quad in range(4):
                for j in range(4):
                    joined[
                        pl.ds(64 * core + SPAN * at, SPAN), pl.ds((4 * quad + j) * HD, HD)
                    ] = attended[core, 4 * at + quad, pl.ds(SPAN * j, SPAN), :]
    for pair in range(2):
        product = jnp.dot(
            joined[...], weight[:, pl.ds(2 * HD * pair, 2 * HD)], preferred_element_type=F32
        ).astype(BF16)
        out[2 * pair] = product[:, :HD]
        out[2 * pair + 1] = product[:, HD:]


def update_kernel(shares, residual, updated, rounded, squares):
    total = residual[...].astype(F32)
    for i in range(shares.shape[0]):
        total += shares[i].astype(F32)
    updated[...] = total
    rounded[...] = total.astype(BF16)
    own = jnp.sum(total * total, axis=1, keepdims=True)
    row = jnp.broadcast_to(own, total.shape).T[0:8]
    for i in range(squares.shape[0] // 8):
        squares[pl.ds(8 * i, 8), :] = row


def norm_kernel(width, updated, squares, gain, out):
    total = jnp.sum(squares[...], axis=0, keepdims=True)
    factor = lax.rsqrt(total / width + EPSILON)
    column = jnp.broadcast_to(factor, updated.shape).T
    out[...] = (updated[...] * column * gain[...]).astype(BF16)


def on_device(queries, cache_keys, cache_values, prefix_lengths, residual_in, out_weight, norm_gain):
    chips = lax.axis_size("y")
    pipes = lax.axis_size("pipe")
    devices = 2 * chips * pipes
    tokens = queries.shape[0]
    slots = cache_keys.shape[1]
    core = lax.axis_index("core")
    chip = lax.axis_index("y")
    place = jnp.stack([core, (2 * chip + core) * slots, (2 * chip + 1 - core) * slots]).astype(jnp.int32)

    halves = jnp.broadcast_to(queries.reshape(1, 2, tokens // 2, HD), (chips, 2, tokens // 2, HD))
    gathered = lax.all_to_all(
        halves.reshape(2 * chips, tokens // 2, HD), ("y", "core"), 0, 0, tiled=True
    )
    away = jnp.stack(
        [lax.dynamic_slice_in_dim(a, 2 * (1 - core), 2, axis=0) for a in (cache_keys, cache_values)]
    )
    others = lax.ppermute(away, "core", [(0, 1), (1, 0)])

    parts = call(
        attend_kernel,
        jax.ShapeDtypeStruct((chips, HD + STATS, HD), BF16),
        (place, prefix_lengths, gathered, cache_keys, cache_values, others),
        in_specs=[SMEM, SMEM, VMEM, VMEM, VMEM, VMEM],
        flops=4 * 2 * 2 * 512 * 256 * HD,
        moved=2**21,
        name="attend",
    )
    parts = lax.all_to_all(parts, "y", 0, 0, tiled=True)
    own = call(
        combine_kernel,
        jax.ShapeDtypeStruct((chips, HD, HD), BF16),
        (parts,),
        flops=2 * 8 * HD * HD,
        moved=2**19,
        name="combine",
    )
    half = lax.all_to_all(own, "y", 0, 0, tiled=True)
    attended = lax.all_gather(half, "core")

    depth, groups, width = out_weight.shape
    shares = call(
        project_kernel,
        jax.ShapeDtypeStruct((groups, tokens, width), BF16),
        (attended, out_weight.reshape(depth, groups * width)),
        scratch=[pltpu.VMEM((tokens, depth), BF16)],
        flops=2 * tokens * depth * groups * width,
        moved=3 * 2**20,
        name="project",
    )
    shares = lax.all_to_all(shares, "pipe", 0, 0, tiled=True)
    updated, rounded, squares = call(
        update_kernel,
        (
            jax.ShapeDtypeStruct((tokens, width), F32),
            jax.ShapeDtypeStruct((tokens, width), BF16),
            jax.ShapeDtypeStruct((devices, tokens), F32),
        ),
        (shares, residual_in),
        flops=8 * tokens * width,
        moved=2**18,
        name="update",
    )
    squares = lax.all_to_all(
        squares.reshape(devices, 1, tokens), ("pipe", "y", "core"), 0, 0, tiled=True
    ).reshape(devices, tokens)

    normed = call(
        lambda *refs: norm_kernel(devices * width, *refs),
        jax.ShapeDtypeStruct((tokens, width), BF16),
        (updated, squares, norm_gain.reshape(1, width)),
        flops=4 * tokens * width,
        moved=2**18,
        name="norm",
    )
    return rounded, normed


def solution(mesh):
    replica, pipe, tensor = mesh.devices.shape
    mesh = Mesh(
        mesh.devices.reshape(replica, pipe, tensor // 2, 2), ("replica", "pipe", "y", "core")
    )
    features = ("pipe", "y", "core")
    tensor = ("y", "core")
    in_specs = (
        P("replica", features),
        P("replica", tensor, "pipe"),
        P("replica", tensor, "pipe"),
        P("replica"),
        P("replica", features),
        P("pipe", None, tensor),
        P(features),
    )
    out_specs = (P("replica", features), P("replica", features))
    return jax.shard_map(
        on_device, mesh=mesh, in_specs=in_specs, out_specs=out_specs, check_vma=False
    )
```

```python
import math

import jax
import jax.numpy as jnp
from jax import lax
from jax.experimental import pallas as pl
from jax.experimental.pallas import tpu as pltpu
from jax.sharding import Mesh
from jax.sharding import PartitionSpec as P

HD = 128
SPAN = 32
MASKED = -1e30
FLOOR = -1e29
EPSILON = 1e-05
STATS = 16

VMEM = pl.BlockSpec(memory_space=pltpu.VMEM)
SMEM = pl.BlockSpec(memory_space=pltpu.SMEM)
F32 = jnp.float32
BF16 = jnp.bfloat16


def call(kernel, out_shape, args, in_specs=None, scratch=(), flops=0, moved=0, name=None):
    return pl.pallas_call(
        kernel,
        out_shape=out_shape,
        in_specs=in_specs or [VMEM] * len(args),
        out_specs=jax.tree.map(lambda _: VMEM, out_shape),
        scratch_shapes=list(scratch),
        compiler_params=pltpu.CompilerParams(vmem_limit_bytes=24 * 2**20),
        cost_estimate=pl.CostEstimate(flops=flops, bytes_accessed=moved, transcendentals=0),
        name=name,
    )(*args)


def arrange_kernel(queries, out):
    heads = queries.shape[0] // 2
    rows = heads * SPAN
    blank = jnp.zeros((rows, HD), BF16)
    for request in range(out.shape[0]):
        for group in range(2):
            for of in range(2):
                out[request, pl.ds(rows * group, rows), pl.ds(HD * of, HD)] = (
                    queries[pl.ds(heads * group, heads), pl.ds(SPAN * request, SPAN), :].reshape(rows, HD)
                    if of == group
                    else blank
                )


def attend_kernel(place, prefix, queries, keys, values, other_keys, other_values, weight, out):
    del weight
    starts = (place[0], place[1])
    requests, slots, width = keys.shape
    rows = width
    ahead = lax.broadcasted_iota(jnp.int32, (slots, rows), 0) - lax.rem(
        lax.broadcasted_iota(jnp.int32, (slots, rows), 1), SPAN
    )
    line = lax.broadcasted_iota(jnp.int32, (STATS, rows), 0)
    scale = math.log2(math.e) / math.sqrt(HD)
    for request in range(requests):
        wanted = queries[request]
        scores = []
        for key, start in zip((keys, other_keys), starts):
            score = lax.dot_general(
                key[request], wanted, (((1,), (1,)), ((), ())), preferred_element_type=F32
            )
            scores.append(jnp.where(ahead <= prefix[request] - start, score * scale, MASKED))
        peak = jnp.maximum(*[jnp.max(s, axis=0, keepdims=True) for s in scores])
        peak = jnp.maximum(peak, FLOOR).astype(BF16).astype(F32)
        weights = [jnp.exp2(s - peak) for s in scores]
        total = sum(jnp.sum(w, axis=0, keepdims=True) for w in weights)
        summed = sum(
            lax.dot_general(
                value[request], w.astype(BF16), (((0,), (0,)), ((), ())), preferred_element_type=F32
            )
            for value, w in zip((values, other_values), weights)
        )
        inverse = jnp.where(total > 0, 1.0 / total, 0.0)
        high = total.astype(BF16).astype(F32)
        stats = jnp.where(
            line == 0, peak, jnp.where(line == 1, high, jnp.where(line == 2, total - high, 0.0))
        ).astype(BF16)
        for group in range(2):
            part = slice(group * HD, (group + 1) * HD)
            out[2 * request + group, pl.ds(0, HD), :] = (summed[part, part] * inverse[:, part]).astype(BF16)
            out[2 * request + group, pl.ds(HD, STATS), :] = stats[:, part]


def combine_kernel(parts, out):
    count = parts.shape[0]
    stats = [parts[i, pl.ds(HD, STATS), :].astype(F32) for i in range(count)]
    peaks = [s[0:1] for s in stats]
    overall = peaks[0]
    for peak in peaks[1:]:
        overall = jnp.maximum(overall, peak)
    shares = [(s[1:2] + s[2:3]) * jnp.exp2(p - overall) for s, p in zip(stats, peaks)]
    inverse = 1.0 / sum(shares)
    summed = jnp.zeros((HD, HD), F32)
    for i in range(count):
        summed += parts[i, pl.ds(0, HD), :].astype(F32) * (shares[i] * inverse)
    attended = summed.T.astype(BF16)
    for i in range(count):
        out[i] = attended


def project_kernel(attended, weight, out, joined):
    for core in range(2):
        for place in range(attended.shape[1]):
            request, group = place // 2, place % 2
            for j in range(4):
                joined[
                    pl.ds(SPAN * request, SPAN), pl.ds((8 * group + 2 * j + core) * HD, HD)
                ] = attended[core, place, pl.ds(SPAN * j, SPAN), :]
    for pair in range(2):
        product = jnp.dot(
            joined[...], weight[:, pl.ds(2 * HD * pair, 2 * HD)], preferred_element_type=F32
        ).astype(BF16)
        out[2 * pair] = product[:, :HD]
        out[2 * pair + 1] = product[:, HD:]


def update_kernel(shares, residual, updated, rounded, squares):
    total = residual[...].astype(F32)
    for i in range(shares.shape[0]):
        total += shares[i].astype(F32)
    updated[...] = total
    rounded[...] = total.astype(BF16)
    own = jnp.sum(total * total, axis=1, keepdims=True)
    row = jnp.broadcast_to(own, total.shape).T[0:8]
    for i in range(squares.shape[0] // 8):
        squares[pl.ds(8 * i, 8), :] = row


def norm_kernel(width, updated, squares, gain, out):
    total = jnp.sum(squares[...], axis=0, keepdims=True)
    factor = lax.rsqrt(total / width + EPSILON)
    column = jnp.broadcast_to(factor, updated.shape).T
    out[...] = (updated[...] * column * gain[...]).astype(BF16)


def on_device(queries, cache_keys, cache_values, prefix_lengths, residual_in, out_weight, norm_gain):
    chips = lax.axis_size("y")
    pipes = lax.axis_size("pipe")
    devices = 2 * chips * pipes
    tokens = queries.shape[0]
    slots = cache_keys.shape[1]
    depth, groups, width = out_weight.shape
    weight = out_weight.reshape(depth, groups * width)
    core = lax.axis_index("core")
    chip = lax.axis_index("y")
    place = jnp.stack([(2 * chip + core) * slots, (2 * chip + 1 - core) * slots]).astype(jnp.int32)

    gathered = lax.all_to_all(
        jnp.broadcast_to(queries, (chips, tokens, HD)), "y", 0, 0, tiled=True
    )
    swap = [(0, 1), (1, 0)]
    other_keys = lax.ppermute(cache_keys, "core", swap)
    other_values = lax.ppermute(cache_values, "core", swap)

    arranged = call(
        arrange_kernel,
        jax.ShapeDtypeStruct((cache_keys.shape[0], 2 * HD, 2 * HD), BF16),
        (gathered,),
        flops=2**30,
        moved=2**19,
        name="arrange",
    )
    parts = call(
        attend_kernel,
        jax.ShapeDtypeStruct((chips, HD + STATS, HD), BF16),
        (place, prefix_lengths, arranged, cache_keys, cache_values, other_keys, other_values, weight),
        in_specs=[SMEM, SMEM] + [VMEM] * 5 + [pl.BlockSpec(memory_space=pl.ANY)],
        flops=4 * 2 * 2 * 512 * 256 * HD,
        moved=2**21,
        name="attend",
    )
    parts = lax.all_to_all(parts, "y", 0, 0, tiled=True)
    own = call(
        combine_kernel,
        jax.ShapeDtypeStruct((chips, HD, HD), BF16),
        (parts,),
        flops=2 * 8 * HD * HD,
        moved=2**19,
        name="combine",
    )
    half = lax.all_to_all(own, "y", 0, 0, tiled=True)
    attended = lax.all_gather(half, "core")

    shares = call(
        project_kernel,
        jax.ShapeDtypeStruct((groups, tokens, width), BF16),
        (attended.reshape(2, chips, HD, HD), weight),
        scratch=[pltpu.VMEM((tokens, depth), BF16)],
        flops=2 * tokens * depth * groups * width,
        moved=3 * 2**20,
        name="project",
    )
    shares = lax.all_to_all(shares, "pipe", 0, 0, tiled=True)
    updated, rounded, squares = call(
        update_kernel,
        (
            jax.ShapeDtypeStruct((tokens, width), F32),
            jax.ShapeDtypeStruct((tokens, width), BF16),
            jax.ShapeDtypeStruct((devices, tokens), F32),
        ),
        (shares, residual_in),
        flops=8 * tokens * width,
        moved=2**18,
        name="update",
    )
    squares = lax.all_to_all(
        squares.reshape(devices, 1, tokens), ("pipe", "y", "core"), 0, 0, tiled=True
    ).reshape(devices, tokens)

    normed = call(
        lambda *refs: norm_kernel(devices * width, *refs),
        jax.ShapeDtypeStruct((tokens, width), BF16),
        (updated, squares, norm_gain.reshape(1, width)),
        flops=4 * tokens * width,
        moved=2**18,
        name="norm",
    )
    return rounded, normed


def solution(mesh):
    replica, pipe, tensor = mesh.devices.shape
    mesh = Mesh(
        mesh.devices.reshape(replica, pipe, tensor // 2, 2), ("replica", "pipe", "y", "core")
    )
    features = ("pipe", "y", "core")
    tensor = ("y", "core")
    in_specs = (
        P("replica", features),
        P("replica", tensor, "pipe"),
        P("replica", tensor, "pipe"),
        P("replica"),
        P("replica", features),
        P("pipe", None, tensor),
        P(features),
    )
    out_specs = (P("replica", features), P("replica", features))
    return jax.shard_map(
        on_device, mesh=mesh, in_specs=in_specs, out_specs=out_specs, check_vma=False
    )
```

```python
import math

import jax
import jax.numpy as jnp
from jax import lax
from jax.experimental import pallas as pl
from jax.experimental.pallas import tpu as pltpu
from jax.sharding import Mesh
from jax.sharding import PartitionSpec as P

HD = 128
SPAN = 32
MASKED = -1e30
FLOOR = -1e29
EPSILON = 1e-05
STATS = 16

VMEM = pl.BlockSpec(memory_space=pltpu.VMEM)
F32 = jnp.float32
BF16 = jnp.bfloat16


def call(kernel, out_shape, args, in_specs=None, scratch=(), flops=0, moved=0, name=None):
    return pl.pallas_call(
        kernel,
        out_shape=out_shape,
        in_specs=in_specs or [VMEM] * len(args),
        out_specs=jax.tree.map(lambda _: VMEM, out_shape),
        scratch_shapes=list(scratch),
        compiler_params=pltpu.CompilerParams(vmem_limit_bytes=24 * 2**20),
        cost_estimate=pl.CostEstimate(flops=flops, bytes_accessed=moved, transcendentals=0),
        name=name,
    )(*args)


def arrange_kernel(queries, out):
    heads = queries.shape[0] // 2
    rows = heads * SPAN
    blank = jnp.zeros((rows, HD), BF16)
    for request in range(out.shape[0]):
        for group in range(2):
            for of in range(2):
                out[request, pl.ds(rows * group, rows), pl.ds(HD * of, HD)] = (
                    queries[pl.ds(heads * group, heads), pl.ds(SPAN * request, SPAN), :].reshape(rows, HD)
                    if of == group
                    else blank
                )


def attend_kernel(prefix, queries, keys, values, other_keys, other_values, out):
    requests, slots, width = keys.shape
    rows = width
    slot = lax.broadcasted_iota(jnp.int32, (slots, rows), 0)
    line = lax.broadcasted_iota(jnp.int32, (STATS, rows), 0)
    lane = lax.rem(lax.broadcasted_iota(jnp.int32, (1, rows), 1), SPAN)
    core = lax.axis_index("core")
    chunk = 2 * lax.axis_index("y") + core
    offsets = (lane - chunk * slots, lane - (chunk + 1 - 2 * core) * slots)
    scale = math.log2(math.e) / math.sqrt(HD)
    for request in range(requests):
        wanted = queries[request]
        scores = []
        for key, offset in zip((keys, other_keys), offsets):
            score = lax.dot_general(
                key[request], wanted, (((1,), (1,)), ((), ())), preferred_element_type=F32
            )
            visible = slot <= prefix[:, request : request + 1] + offset
            scores.append(jnp.where(visible, score * scale, MASKED))
        peak = jnp.maximum(*[jnp.max(s, axis=0, keepdims=True) for s in scores])
        peak = jnp.maximum(peak, FLOOR).astype(BF16).astype(F32)
        weights = [jnp.exp2(s - peak) for s in scores]
        total = sum(jnp.sum(w, axis=0, keepdims=True) for w in weights)
        summed = sum(
            lax.dot_general(
                value[request], w.astype(BF16), (((0,), (0,)), ((), ())), preferred_element_type=F32
            )
            for value, w in zip((values, other_values), weights)
        )
        inverse = jnp.where(total > 0, 1.0 / total, 0.0)
        high = total.astype(BF16).astype(F32)
        stats = jnp.where(
            line == 0, peak, jnp.where(line == 1, high, jnp.where(line == 2, total - high, 0.0))
        ).astype(BF16)
        for group in range(2):
            part = slice(group * HD, (group + 1) * HD)
            out[2 * request + group, pl.ds(0, HD), :] = (summed[part, part] * inverse[:, part]).astype(BF16)
            out[2 * request + group, pl.ds(HD, STATS), :] = stats[:, part]


def combine_kernel(parts, weight, out):
    del weight
    count = parts.shape[0]
    stats = [parts[i, pl.ds(HD, STATS), :].astype(F32) for i in range(count)]
    peaks = [s[0:1] for s in stats]
    overall = peaks[0]
    for peak in peaks[1:]:
        overall = jnp.maximum(overall, peak)
    shares = [(s[1:2] + s[2:3]) * jnp.exp2(p - overall) for s, p in zip(stats, peaks)]
    inverse = 1.0 / sum(shares)
    summed = jnp.zeros((HD, HD), F32)
    for i in range(count):
        summed += parts[i, pl.ds(0, HD), :].astype(F32) * (shares[i] * inverse)
    attended = summed.T.astype(BF16)
    for i in range(count):
        out[i] = attended


def project_kernel(attended, weight, out, joined):
    for core in range(2):
        for place in range(attended.shape[1]):
            request, group = place // 2, place % 2
            for j in range(4):
                joined[
                    pl.ds(SPAN * request, SPAN), pl.ds((8 * group + 2 * j + core) * HD, HD)
                ] = attended[core, place, pl.ds(SPAN * j, SPAN), :]
    for pair in range(2):
        product = jnp.dot(
            joined[...], weight[:, pl.ds(2 * HD * pair, 2 * HD)], preferred_element_type=F32
        ).astype(BF16)
        out[2 * pair] = product[:, :HD]
        out[2 * pair + 1] = product[:, HD:]


def update_kernel(shares, residual, updated, squares):
    total = residual[...].astype(F32)
    for i in range(shares.shape[0]):
        total += shares[i].astype(F32)
    updated[...] = total
    own = jnp.sum(total * total, axis=1, keepdims=True)
    row = jnp.broadcast_to(own, total.shape).T[0:8]
    for i in range(squares.shape[0] // 8):
        squares[pl.ds(8 * i, 8), :] = row


def norm_kernel(width, updated, squares, gain, rounded, out):
    rounded[...] = updated[...].astype(BF16)
    total = jnp.sum(squares[...], axis=0, keepdims=True)
    factor = lax.rsqrt(total / width + EPSILON)
    column = jnp.broadcast_to(factor, updated.shape).T
    out[...] = (updated[...] * column * gain[...]).astype(BF16)


def on_device(queries, cache_keys, cache_values, prefix_lengths, residual_in, out_weight, norm_gain):
    chips = lax.axis_size("y")
    pipes = lax.axis_size("pipe")
    devices = 2 * chips * pipes
    tokens = queries.shape[0]
    depth, groups, width = out_weight.shape
    weight = out_weight.reshape(depth, groups * width)
    gathered = lax.all_to_all(
        jnp.broadcast_to(queries, (chips, tokens, HD)), "y", 0, 0, tiled=True
    )
    swap = [(0, 1), (1, 0)]
    other_keys = lax.ppermute(cache_keys, "core", swap)
    other_values = lax.ppermute(cache_values, "core", swap)

    arranged = call(
        arrange_kernel,
        jax.ShapeDtypeStruct((cache_keys.shape[0], 2 * HD, 2 * HD), BF16),
        (gathered,),
        flops=2**30,
        moved=2**19,
        name="arrange",
    )
    parts = call(
        attend_kernel,
        jax.ShapeDtypeStruct((chips, HD + STATS, HD), BF16),
        (prefix_lengths.reshape(1, -1), arranged, cache_keys, cache_values, other_keys, other_values),
        in_specs=[VMEM] * 6,
        flops=4 * 2 * 2 * 512 * 256 * HD,
        moved=2**21,
        name="attend",
    )
    parts = lax.all_to_all(parts, "y", 0, 0, tiled=True)
    own = call(
        combine_kernel,
        jax.ShapeDtypeStruct((chips, HD, HD), BF16),
        (parts, weight),
        in_specs=[VMEM, pl.BlockSpec(memory_space=pl.ANY)],
        flops=2 * 8 * HD * HD,
        moved=2**19,
        name="combine",
    )
    half = lax.all_to_all(own, "y", 0, 0, tiled=True)
    attended = lax.all_gather(half, "core")

    shares = call(
        project_kernel,
        jax.ShapeDtypeStruct((groups, tokens, width), BF16),
        (attended.reshape(2, chips, HD, HD), weight),
        scratch=[pltpu.VMEM((tokens, depth), BF16)],
        flops=2 * tokens * depth * groups * width,
        moved=3 * 2**20,
        name="project",
    )
    shares = lax.all_to_all(shares, "pipe", 0, 0, tiled=True)
    updated, squares = call(
        update_kernel,
        (
            jax.ShapeDtypeStruct((tokens, width), F32),
            jax.ShapeDtypeStruct((devices, tokens), F32),
        ),
        (shares, residual_in),
        flops=8 * tokens * width,
        moved=2**18,
        name="update",
    )
    squares = lax.all_to_all(
        squares.reshape(devices, 1, tokens), ("pipe", "y", "core"), 0, 0, tiled=True
    ).reshape(devices, tokens)

    return call(
        lambda *refs: norm_kernel(devices * width, *refs),
        (jax.ShapeDtypeStruct((tokens, width), BF16),) * 2,
        (updated, squares, norm_gain.reshape(1, width)),
        flops=4 * tokens * width,
        moved=2**18,
        name="norm",
    )


def solution(mesh):
    replica, pipe, tensor = mesh.devices.shape
    mesh = Mesh(
        mesh.devices.reshape(replica, pipe, tensor // 2, 2), ("replica", "pipe", "y", "core")
    )
    features = ("pipe", "y", "core")
    tensor = ("y", "core")
    in_specs = (
        P("replica", features),
        P("replica", tensor, "pipe"),
        P("replica", tensor, "pipe"),
        P("replica"),
        P("replica", features),
        P("pipe", None, tensor),
        P(features),
    )
    out_specs = (P("replica", features), P("replica", features))
    return jax.shard_map(
        on_device, mesh=mesh, in_specs=in_specs, out_specs=out_specs, check_vma=False
    )
```

```python
import math

import jax
import jax.numpy as jnp
from jax import lax
from jax.experimental import pallas as pl
from jax.experimental.pallas import tpu as pltpu
from jax.sharding import Mesh
from jax.sharding import PartitionSpec as P

HD = 128
SPAN = 32
MASKED = -1e30
FLOOR = -1e29
EPSILON = 1e-05
STATS = 16

VMEM = pl.BlockSpec(memory_space=pltpu.VMEM)
F32 = jnp.float32
BF16 = jnp.bfloat16


def call(kernel, out_shape, args, in_specs=None, out_specs=None, scratch=(), flops=0, moved=0, name=None):
    return pl.pallas_call(
        kernel,
        out_shape=out_shape,
        in_specs=in_specs or [VMEM] * len(args),
        out_specs=out_specs or jax.tree.map(lambda _: VMEM, out_shape),
        scratch_shapes=list(scratch),
        compiler_params=pltpu.CompilerParams(vmem_limit_bytes=24 * 2**20),
        cost_estimate=pl.CostEstimate(flops=flops, bytes_accessed=moved, transcendentals=0),
        name=name,
    )(*args)


def arrange_kernel(queries, out):
    heads = queries.shape[0] // 2
    rows = heads * SPAN
    blank = jnp.zeros((rows, HD), BF16)
    for request in range(out.shape[0]):
        for group in range(2):
            for of in range(2):
                out[request, pl.ds(rows * group, rows), pl.ds(HD * of, HD)] = (
                    queries[pl.ds(heads * group, heads), pl.ds(SPAN * request, SPAN), :].reshape(rows, HD)
                    if of == group
                    else blank
                )


def attend_kernel(prefix, queries, keys, values, other_keys, other_values, out, staged, sems):
    requests, slots, width = keys.shape
    rows = width
    slot = lax.broadcasted_iota(jnp.int32, (slots, rows), 0)
    line = lax.broadcasted_iota(jnp.int32, (STATS, rows), 0)
    lane = lax.rem(lax.broadcasted_iota(jnp.int32, (1, rows), 1), SPAN)
    core = lax.axis_index("core")
    chunk = 2 * lax.axis_index("y") + core
    offsets = (lane - chunk * slots, lane - (chunk + 1 - 2 * core) * slots)
    scale = math.log2(math.e) / math.sqrt(HD)
    copies = []
    for request in range(requests):
        wanted = queries[request]
        scores = []
        for key, offset in zip((keys, other_keys), offsets):
            score = lax.dot_general(
                key[request], wanted, (((1,), (1,)), ((), ())), preferred_element_type=F32
            )
            visible = slot <= prefix[:, request : request + 1] + offset
            scores.append(jnp.where(visible, score * scale, MASKED))
        peak = jnp.maximum(*[jnp.max(s, axis=0, keepdims=True) for s in scores])
        peak = jnp.maximum(peak, FLOOR).astype(BF16).astype(F32)
        weights = [jnp.exp2(s - peak) for s in scores]
        total = sum(jnp.sum(w, axis=0, keepdims=True) for w in weights)
        summed = sum(
            lax.dot_general(
                value[request], w.astype(BF16), (((0,), (0,)), ((), ())), preferred_element_type=F32
            )
            for value, w in zip((values, other_values), weights)
        )
        inverse = jnp.where(total > 0, 1.0 / total, 0.0)
        high = total.astype(BF16).astype(F32)
        stats = jnp.where(
            line == 0, peak, jnp.where(line == 1, high, jnp.where(line == 2, total - high, 0.0))
        ).astype(BF16)
        for group in range(2):
            part = slice(group * HD, (group + 1) * HD)
            staged[2 * request + group, pl.ds(0, HD), :] = (summed[part, part] * inverse[:, part]).astype(BF16)
            staged[2 * request + group, pl.ds(HD, STATS), :] = stats[:, part]
        pair = pl.ds(2 * request, 2)
        copies.append(pltpu.make_async_copy(staged.at[pair], out.at[pair], sems.at[request]))
        copies[-1].start()
    for copy in copies:
        copy.wait()


def combine_kernel(parts, weight, out):
    del weight
    count = parts.shape[0]
    stats = [parts[i, pl.ds(HD, STATS), :].astype(F32) for i in range(count)]
    peaks = [s[0:1] for s in stats]
    overall = peaks[0]
    for peak in peaks[1:]:
        overall = jnp.maximum(overall, peak)
    shares = [(s[1:2] + s[2:3]) * jnp.exp2(p - overall) for s, p in zip(stats, peaks)]
    inverse = 1.0 / sum(shares)
    summed = jnp.zeros((HD, HD), F32)
    for i in range(count):
        summed += parts[i, pl.ds(0, HD), :].astype(F32) * (shares[i] * inverse)
    attended = summed.T.astype(BF16)
    for i in range(count):
        out[i] = attended


def project_kernel(attended, weight, out, joined):
    for core in range(2):
        for place in range(attended.shape[1]):
            request, group = place // 2, place % 2
            for j in range(4):
                joined[
                    pl.ds(SPAN * request, SPAN), pl.ds((8 * group + 2 * j + core) * HD, HD)
                ] = attended[core, place, pl.ds(SPAN * j, SPAN), :]
    for pair in range(2):
        product = jnp.dot(
            joined[...], weight[:, pl.ds(2 * HD * pair, 2 * HD)], preferred_element_type=F32
        ).astype(BF16)
        out[2 * pair] = product[:, :HD]
        out[2 * pair + 1] = product[:, HD:]


def update_kernel(shares, residual, updated, squares):
    total = residual[...].astype(F32)
    for i in range(shares.shape[0]):
        total += shares[i].astype(F32)
    updated[...] = total
    own = jnp.sum(total * total, axis=1, keepdims=True)
    row = jnp.broadcast_to(own, total.shape).T[0:8]
    for i in range(squares.shape[0] // 8):
        squares[pl.ds(8 * i, 8), :] = row


def norm_kernel(width, updated, squares, gain, rounded, out):
    rounded[...] = updated[...].astype(BF16)
    total = jnp.sum(squares[...], axis=0, keepdims=True)
    factor = lax.rsqrt(total / width + EPSILON)
    column = jnp.broadcast_to(factor, updated.shape).T
    out[...] = (updated[...] * column * gain[...]).astype(BF16)


def on_device(queries, cache_keys, cache_values, prefix_lengths, residual_in, out_weight, norm_gain):
    chips = lax.axis_size("y")
    pipes = lax.axis_size("pipe")
    devices = 2 * chips * pipes
    tokens = queries.shape[0]
    depth, groups, width = out_weight.shape
    weight = out_weight.reshape(depth, groups * width)
    gathered = lax.all_to_all(
        jnp.broadcast_to(queries, (chips, tokens, HD)), "y", 0, 0, tiled=True
    )
    swap = [(0, 1), (1, 0)]
    other_keys = lax.ppermute(cache_keys, "core", swap)
    other_values = lax.ppermute(cache_values, "core", swap)

    arranged = call(
        arrange_kernel,
        jax.ShapeDtypeStruct((cache_keys.shape[0], 2 * HD, 2 * HD), BF16),
        (gathered,),
        flops=2**30,
        moved=2**19,
        name="arrange",
    )
    parts = call(
        attend_kernel,
        jax.ShapeDtypeStruct((chips, HD + STATS, HD), BF16),
        (prefix_lengths.reshape(1, -1), arranged, cache_keys, cache_values, other_keys, other_values),
        out_specs=pl.BlockSpec(memory_space=pl.ANY),
        scratch=[
            pltpu.VMEM((chips, HD + STATS, HD), BF16),
            pltpu.SemaphoreType.DMA((cache_keys.shape[0],)),
        ],
        flops=4 * 2 * 2 * 512 * 256 * HD,
        moved=2**21,
        name="attend",
    )
    parts = lax.all_to_all(parts, "y", 0, 0, tiled=True)
    own = call(
        combine_kernel,
        jax.ShapeDtypeStruct((chips, HD, HD), BF16),
        (parts, weight),
        in_specs=[VMEM, pl.BlockSpec(memory_space=pl.ANY)],
        flops=2 * 8 * HD * HD,
        moved=2**19,
        name="combine",
    )
    half = lax.all_to_all(own, "y", 0, 0, tiled=True)
    attended = lax.all_gather(half, "core")

    shares = call(
        project_kernel,
        jax.ShapeDtypeStruct((groups, tokens, width), BF16),
        (attended.reshape(2, chips, HD, HD), weight),
        scratch=[pltpu.VMEM((tokens, depth), BF16)],
        flops=2 * tokens * depth * groups * width,
        moved=3 * 2**20,
        name="project",
    )
    shares = lax.all_to_all(shares, "pipe", 0, 0, tiled=True)
    updated, squares = call(
        update_kernel,
        (
            jax.ShapeDtypeStruct((tokens, width), F32),
            jax.ShapeDtypeStruct((devices, tokens), F32),
        ),
        (shares, residual_in),
        flops=8 * tokens * width,
        moved=2**18,
        name="update",
    )
    squares = lax.all_to_all(
        squares.reshape(devices, 1, tokens), ("pipe", "y", "core"), 0, 0, tiled=True
    ).reshape(devices, tokens)

    return call(
        lambda *refs: norm_kernel(devices * width, *refs),
        (jax.ShapeDtypeStruct((tokens, width), BF16),) * 2,
        (updated, squares, norm_gain.reshape(1, width)),
        flops=4 * tokens * width,
        moved=2**18,
        name="norm",
    )


def solution(mesh):
    replica, pipe, tensor = mesh.devices.shape
    mesh = Mesh(
        mesh.devices.reshape(replica, pipe, tensor // 2, 2), ("replica", "pipe", "y", "core")
    )
    features = ("pipe", "y", "core")
    tensor = ("y", "core")
    in_specs = (
        P("replica", features),
        P("replica", tensor, "pipe"),
        P("replica", tensor, "pipe"),
        P("replica"),
        P("replica", features),
        P("pipe", None, tensor),
        P(features),
    )
    out_specs = (P("replica", features), P("replica", features))
    return jax.shard_map(
        on_device, mesh=mesh, in_specs=in_specs, out_specs=out_specs, check_vma=False
    )
```

```python
import math

import jax
import jax.numpy as jnp
from jax import lax
from jax.experimental import pallas as pl
from jax.experimental.pallas import tpu as pltpu
from jax.sharding import Mesh
from jax.sharding import PartitionSpec as P

HD = 128
SPAN = 32
MASKED = -1e30
FLOOR = -1e29
EPSILON = 1e-05
STATS = 16

VMEM = pl.BlockSpec(memory_space=pltpu.VMEM)
F32 = jnp.float32
BF16 = jnp.bfloat16


def call(kernel, out_shape, args, in_specs=None, out_specs=None, scratch=(), flops=0, moved=0, name=None):
    return pl.pallas_call(
        kernel,
        out_shape=out_shape,
        in_specs=in_specs or [VMEM] * len(args),
        out_specs=out_specs or jax.tree.map(lambda _: VMEM, out_shape),
        scratch_shapes=list(scratch),
        compiler_params=pltpu.CompilerParams(vmem_limit_bytes=24 * 2**20),
        cost_estimate=pl.CostEstimate(flops=flops, bytes_accessed=moved, transcendentals=0),
        name=name,
    )(*args)


def arrange_kernel(queries, out):
    heads = queries.shape[0] // 2
    rows = heads * SPAN
    blank = jnp.zeros((rows, HD), BF16)
    for request in range(out.shape[0]):
        for group in range(2):
            for of in range(2):
                out[request, pl.ds(rows * group, rows), pl.ds(HD * of, HD)] = (
                    queries[pl.ds(heads * group, heads), pl.ds(SPAN * request, SPAN), :].reshape(rows, HD)
                    if of == group
                    else blank
                )


def attend_kernel(prefix, queries, keys, values, other_keys, other_values, out, staged, sems):
    requests, slots, width = keys.shape
    rows = width
    slot = lax.broadcasted_iota(jnp.int32, (slots, rows), 0)
    line = lax.broadcasted_iota(jnp.int32, (STATS, rows), 0)
    lane = lax.rem(lax.broadcasted_iota(jnp.int32, (1, rows), 1), SPAN)
    core = lax.axis_index("core")
    chunk = 2 * lax.axis_index("y") + core
    offsets = (lane - chunk * slots, lane - (chunk + 1 - 2 * core) * slots)
    scale = math.log2(math.e) / math.sqrt(HD)
    copies = []
    for request in range(requests):
        wanted = queries[request]
        scores = []
        for key, offset in zip((keys, other_keys), offsets):
            score = lax.dot_general(
                key[request], wanted, (((1,), (1,)), ((), ())), preferred_element_type=F32
            )
            visible = slot <= prefix[:, request : request + 1] + offset
            scores.append(jnp.where(visible, score * scale, MASKED))
        peak = jnp.maximum(*[jnp.max(s, axis=0, keepdims=True) for s in scores])
        peak = jnp.maximum(peak, FLOOR).astype(BF16).astype(F32)
        weights = [jnp.exp2(s - peak) for s in scores]
        total = sum(jnp.sum(w, axis=0, keepdims=True) for w in weights)
        summed = sum(
            lax.dot_general(
                value[request], w.astype(BF16), (((0,), (0,)), ((), ())), preferred_element_type=F32
            )
            for value, w in zip((values, other_values), weights)
        )
        inverse = jnp.where(total > 0, 1.0 / total, 0.0)
        high = total.astype(BF16).astype(F32)
        stats = jnp.where(
            line == 0, peak, jnp.where(line == 1, high, jnp.where(line == 2, total - high, 0.0))
        ).astype(BF16)
        for group in range(2):
            part = slice(group * HD, (group + 1) * HD)
            staged[2 * request + group, pl.ds(0, HD), :] = (summed[part, part] * inverse[:, part]).astype(BF16)
            staged[2 * request + group, pl.ds(HD, STATS), :] = stats[:, part]
        pair = pl.ds(2 * request, 2)
        copies.append(pltpu.make_async_copy(staged.at[pair], out.at[pair], sems.at[request]))
        copies[-1].start()
    for copy in copies:
        copy.wait()


def combine_kernel(parts, weight, out):
    del weight
    count = parts.shape[0]
    stats = [parts[i, pl.ds(HD, STATS), :].astype(F32) for i in range(count)]
    peaks = [s[0:1] for s in stats]
    overall = peaks[0]
    for peak in peaks[1:]:
        overall = jnp.maximum(overall, peak)
    shares = [(s[1:2] + s[2:3]) * jnp.exp2(p - overall) for s, p in zip(stats, peaks)]
    inverse = 1.0 / sum(shares)
    summed = jnp.zeros((HD, HD), F32)
    for i in range(count):
        summed += parts[i, pl.ds(0, HD), :].astype(F32) * (shares[i] * inverse)
    attended = summed.T.astype(BF16)
    for i in range(count):
        out[i] = attended


def project_kernel(attended, weight, residual, out, own, joined):
    pipe = lax.axis_index("pipe")
    width = residual.shape[1]
    added = residual[...].astype(F32)
    mine = added
    for core in range(2):
        for place in range(attended.shape[1]):
            request, group = place // 2, place % 2
            for j in range(4):
                joined[
                    pl.ds(SPAN * request, SPAN), pl.ds((8 * group + 2 * j + core) * HD, HD)
                ] = attended[core, place, pl.ds(SPAN * j, SPAN), :]
    for pair in range(2):
        product = jnp.dot(
            joined[...], weight[:, pl.ds(2 * width * pair, 2 * width)], preferred_element_type=F32
        )
        for of in range(2):
            group = 2 * pair + of
            share = product[:, of * width : (of + 1) * width].astype(BF16).astype(F32)
            here = jnp.where(pipe == group, 1.0, 0.0)
            mine += share * here
            sent = (share + added * here).astype(BF16)
            for to in range(out.shape[0]):
                out[to, :, pl.ds(group * width, width)] = sent
    own[...] = mine


def update_kernel(shares, own, updated, squares):
    pipe = lax.axis_index("pipe")
    width = own.shape[1]
    total = own[...]
    square = jnp.zeros_like(total)
    for i in range(shares.shape[0]):
        away = jnp.where(pipe == i, 0.0, 1.0)
        block = pl.ds(pl.multiple_of(pipe * width, width), width)
        total += shares[i, :, block].astype(F32) * away
        other = sum(
            shares[j, :, pl.ds(i * width, width)].astype(F32) for j in range(shares.shape[0])
        )
        square += other * other * away
    updated[...] = total
    square = jnp.sum(square + total * total, axis=1, keepdims=True)
    row = jnp.broadcast_to(square, total.shape).T[0:8]
    for i in range(squares.shape[0] // 8):
        squares[pl.ds(8 * i, 8), :] = row


def norm_kernel(width, updated, squares, gain, rounded, out):
    rounded[...] = updated[...].astype(BF16)
    total = jnp.sum(squares[...], axis=0, keepdims=True)
    factor = lax.rsqrt(total / width + EPSILON)
    column = jnp.broadcast_to(factor, updated.shape).T
    out[...] = (updated[...] * column * gain[...]).astype(BF16)


def on_device(queries, cache_keys, cache_values, prefix_lengths, residual_in, out_weight, norm_gain):
    chips = lax.axis_size("y")
    pipes = lax.axis_size("pipe")
    devices = 2 * chips * pipes
    tokens = queries.shape[0]
    depth, groups, width = out_weight.shape
    weight = out_weight.reshape(depth, groups * width)
    gathered = lax.all_to_all(
        jnp.broadcast_to(queries, (chips, tokens, HD)), "y", 0, 0, tiled=True
    )
    swap = [(0, 1), (1, 0)]
    other_keys = lax.ppermute(cache_keys, "core", swap)
    other_values = lax.ppermute(cache_values, "core", swap)

    arranged = call(
        arrange_kernel,
        jax.ShapeDtypeStruct((cache_keys.shape[0], 2 * HD, 2 * HD), BF16),
        (gathered,),
        flops=2**30,
        moved=2**19,
        name="arrange",
    )
    parts = call(
        attend_kernel,
        jax.ShapeDtypeStruct((chips, HD + STATS, HD), BF16),
        (prefix_lengths.reshape(1, -1), arranged, cache_keys, cache_values, other_keys, other_values),
        out_specs=pl.BlockSpec(memory_space=pl.ANY),
        scratch=[
            pltpu.VMEM((chips, HD + STATS, HD), BF16),
            pltpu.SemaphoreType.DMA((cache_keys.shape[0],)),
        ],
        flops=4 * 2 * 2 * 512 * 256 * HD,
        moved=2**21,
        name="attend",
    )
    parts = lax.all_to_all(parts, "y", 0, 0, tiled=True)
    own = call(
        combine_kernel,
        jax.ShapeDtypeStruct((chips, HD, HD), BF16),
        (parts, weight),
        in_specs=[VMEM, pl.BlockSpec(memory_space=pl.ANY)],
        flops=2 * 8 * HD * HD,
        moved=2**19,
        name="combine",
    )
    half = lax.all_to_all(own, "y", 0, 0, tiled=True)
    attended = lax.all_gather(half, "core")

    shares, own = call(
        project_kernel,
        (
            jax.ShapeDtypeStruct((pipes, tokens, groups * width), BF16),
            jax.ShapeDtypeStruct((tokens, width), F32),
        ),
        (attended.reshape(2, chips, HD, HD), weight, residual_in),
        scratch=[pltpu.VMEM((tokens, depth), BF16)],
        flops=2 * tokens * depth * groups * width,
        moved=3 * 2**20,
        name="project",
    )
    shares = lax.all_to_all(shares, "pipe", 0, 0, tiled=True)
    updated, squares = call(
        update_kernel,
        (
            jax.ShapeDtypeStruct((tokens, width), F32),
            jax.ShapeDtypeStruct((2 * chips, tokens), F32),
        ),
        (shares, own),
        flops=8 * tokens * width,
        moved=2**18,
        name="update",
    )
    squares = lax.all_to_all(
        squares.reshape(2 * chips, 1, tokens), ("y", "core"), 0, 0, tiled=True
    ).reshape(2 * chips, tokens)

    return call(
        lambda *refs: norm_kernel(devices * width, *refs),
        (jax.ShapeDtypeStruct((tokens, width), BF16),) * 2,
        (updated, squares, norm_gain.reshape(1, width)),
        flops=4 * tokens * width,
        moved=2**18,
        name="norm",
    )


def solution(mesh):
    replica, pipe, tensor = mesh.devices.shape
    mesh = Mesh(
        mesh.devices.reshape(replica, pipe, tensor // 2, 2), ("replica", "pipe", "y", "core")
    )
    features = ("pipe", "y", "core")
    tensor = ("y", "core")
    in_specs = (
        P("replica", features),
        P("replica", tensor, "pipe"),
        P("replica", tensor, "pipe"),
        P("replica"),
        P("replica", features),
        P("pipe", None, tensor),
        P(features),
    )
    out_specs = (P("replica", features), P("replica", features))
    return jax.shard_map(
        on_device, mesh=mesh, in_specs=in_specs, out_specs=out_specs, check_vma=False
    )
```

```python
import math

import jax
import jax.numpy as jnp
from jax import lax
from jax.experimental import pallas as pl
from jax.experimental.pallas import tpu as pltpu
from jax.sharding import Mesh
from jax.sharding import PartitionSpec as P

HD = 128
SPAN = 32
MASKED = -1e30
FLOOR = -1e29
EPSILON = 1e-05
STATS = 16

VMEM = pl.BlockSpec(memory_space=pltpu.VMEM)
F32 = jnp.float32
BF16 = jnp.bfloat16


def call(kernel, out_shape, args, in_specs=None, out_specs=None, scratch=(), flops=0, moved=0, name=None):
    return pl.pallas_call(
        kernel,
        out_shape=out_shape,
        in_specs=in_specs or [VMEM] * len(args),
        out_specs=out_specs or jax.tree.map(lambda _: VMEM, out_shape),
        scratch_shapes=list(scratch),
        compiler_params=pltpu.CompilerParams(vmem_limit_bytes=24 * 2**20),
        cost_estimate=pl.CostEstimate(flops=flops, bytes_accessed=moved, transcendentals=0),
        name=name,
    )(*args)


def spread_kernel(queries, out):
    for i in range(out.shape[0]):
        out[i] = queries[...]


def arrange_kernel(queries, out):
    heads = queries.shape[0] // 2
    rows = heads * SPAN
    blank = jnp.zeros((rows, HD), BF16)
    for request in range(out.shape[0]):
        for group in range(2):
            for of in range(2):
                out[request, pl.ds(rows * group, rows), pl.ds(HD * of, HD)] = (
                    queries[pl.ds(heads * group, heads), pl.ds(SPAN * request, SPAN), :].reshape(rows, HD)
                    if of == group
                    else blank
                )


def attend_kernel(prefix, queries, keys, values, other_keys, other_values, out, staged, sems):
    requests, slots, width = keys.shape
    rows = width
    slot = lax.broadcasted_iota(jnp.int32, (slots, rows), 0)
    line = lax.broadcasted_iota(jnp.int32, (STATS, rows), 0)
    lane = lax.rem(lax.broadcasted_iota(jnp.int32, (1, rows), 1), SPAN)
    core = lax.axis_index("core")
    chunk = 2 * lax.axis_index("y") + core
    offsets = (lane - chunk * slots, lane - (chunk + 1 - 2 * core) * slots)
    scale = math.log2(math.e) / math.sqrt(HD)
    copies = []
    for request in range(requests):
        wanted = queries[request]
        scores = []
        for key, offset in zip((keys, other_keys), offsets):
            score = lax.dot_general(
                key[request], wanted, (((1,), (1,)), ((), ())), preferred_element_type=F32
            )
            visible = slot <= prefix[:, request : request + 1] + offset
            scores.append(jnp.where(visible, score * scale, MASKED))
        peak = jnp.maximum(*[jnp.max(s, axis=0, keepdims=True) for s in scores])
        peak = jnp.maximum(peak, FLOOR).astype(BF16).astype(F32)
        weights = [jnp.exp2(s - peak) for s in scores]
        total = sum(jnp.sum(w, axis=0, keepdims=True) for w in weights)
        summed = sum(
            lax.dot_general(
                value[request], w.astype(BF16), (((0,), (0,)), ((), ())), preferred_element_type=F32
            )
            for value, w in zip((values, other_values), weights)
        )
        inverse = jnp.where(total > 0, 1.0 / total, 0.0)
        high = total.astype(BF16).astype(F32)
        stats = jnp.where(
            line == 0, peak, jnp.where(line == 1, high, jnp.where(line == 2, total - high, 0.0))
        ).astype(BF16)
        for group in range(2):
            part = slice(group * HD, (group + 1) * HD)
            staged[2 * request + group, pl.ds(0, HD), :] = (summed[part, part] * inverse[:, part]).astype(BF16)
            staged[2 * request + group, pl.ds(HD, STATS), :] = stats[:, part]
            to = 2 * request + group
            copies.append(pltpu.make_async_copy(staged.at[to], out.at[to], sems.at[to]))
            copies[-1].start()
    for copy in copies:
        copy.wait()


def combine_kernel(parts, weight, out):
    del weight
    count = parts.shape[0]
    stats = [parts[i, pl.ds(HD, STATS), :].astype(F32) for i in range(count)]
    peaks = [s[0:1] for s in stats]
    overall = peaks[0]
    for peak in peaks[1:]:
        overall = jnp.maximum(overall, peak)
    shares = [(s[1:2] + s[2:3]) * jnp.exp2(p - overall) for s, p in zip(stats, peaks)]
    inverse = 1.0 / sum(shares)
    summed = jnp.zeros((HD, HD), F32)
    for i in range(count):
        summed += parts[i, pl.ds(0, HD), :].astype(F32) * (shares[i] * inverse)
    attended = summed.T.astype(BF16)
    for i in range(count):
        out[i] = attended


def project_kernel(attended, weight, out, joined):
    for core in range(2):
        for place in range(attended.shape[1]):
            request, group = place // 2, place % 2
            for j in range(4):
                joined[
                    pl.ds(SPAN * request, SPAN), pl.ds((8 * group + 2 * j + core) * HD, HD)
                ] = attended[core, place, pl.ds(SPAN * j, SPAN), :]
    for pair in range(2):
        product = jnp.dot(
            joined[...], weight[:, pl.ds(2 * HD * pair, 2 * HD)], preferred_element_type=F32
        ).astype(BF16)
        out[2 * pair] = product[:, :HD]
        out[2 * pair + 1] = product[:, HD:]


def update_kernel(shares, residual, updated, squares):
    total = residual[...].astype(F32)
    for i in range(shares.shape[0]):
        total += shares[i].astype(F32)
    updated[...] = total
    own = jnp.sum(total * total, axis=1, keepdims=True)
    row = jnp.broadcast_to(own, total.shape).T[0:8]
    for i in range(squares.shape[0] // 8):
        squares[pl.ds(8 * i, 8), :] = row


def norm_kernel(width, updated, squares, gain, rounded, out):
    rounded[...] = updated[...].astype(BF16)
    total = jnp.sum(squares[...], axis=0, keepdims=True)
    factor = lax.rsqrt(total / width + EPSILON)
    column = jnp.broadcast_to(factor, updated.shape).T
    out[...] = (updated[...] * column * gain[...]).astype(BF16)


def on_device(queries, cache_keys, cache_values, prefix_lengths, residual_in, out_weight, norm_gain):
    chips = lax.axis_size("y")
    pipes = lax.axis_size("pipe")
    devices = 2 * chips * pipes
    tokens = queries.shape[0]
    depth, groups, width = out_weight.shape
    weight = out_weight.reshape(depth, groups * width)
    spread = call(
        spread_kernel,
        jax.ShapeDtypeStruct((chips, tokens, HD), BF16),
        (queries,),
        moved=2**18,
        name="spread",
    )
    gathered = lax.all_to_all(
        spread, "y", 0, 0, tiled=True
    )
    swap = [(0, 1), (1, 0)]
    other_keys = lax.ppermute(cache_keys, "core", swap)
    other_values = lax.ppermute(cache_values, "core", swap)

    arranged = call(
        arrange_kernel,
        jax.ShapeDtypeStruct((cache_keys.shape[0], 2 * HD, 2 * HD), BF16),
        (gathered,),
        flops=2**30,
        moved=2**19,
        name="arrange",
    )
    parts = call(
        attend_kernel,
        jax.ShapeDtypeStruct((chips, HD + STATS, HD), BF16),
        (prefix_lengths.reshape(1, -1), arranged, cache_keys, cache_values, other_keys, other_values),
        out_specs=pl.BlockSpec(memory_space=pl.ANY),
        scratch=[
            pltpu.VMEM((chips, HD + STATS, HD), BF16),
            pltpu.SemaphoreType.DMA((chips,)),
        ],
        flops=4 * 2 * 2 * 512 * 256 * HD,
        moved=2**21,
        name="attend",
    )
    parts = lax.all_to_all(parts, "y", 0, 0, tiled=True)
    own = call(
        combine_kernel,
        jax.ShapeDtypeStruct((chips, HD, HD), BF16),
        (parts, weight),
        in_specs=[VMEM, pl.BlockSpec(memory_space=pl.ANY)],
        flops=2 * 8 * HD * HD,
        moved=2**19,
        name="combine",
    )
    half = lax.all_to_all(own, "y", 0, 0, tiled=True)
    attended = lax.all_gather(half, "core")

    shares = call(
        project_kernel,
        jax.ShapeDtypeStruct((groups, tokens, width), BF16),
        (attended.reshape(2, chips, HD, HD), weight),
        scratch=[pltpu.VMEM((tokens, depth), BF16)],
        flops=2 * tokens * depth * groups * width,
        moved=3 * 2**20,
        name="project",
    )
    shares = lax.all_to_all(shares, "pipe", 0, 0, tiled=True)
    updated, squares = call(
        update_kernel,
        (
            jax.ShapeDtypeStruct((tokens, width), F32),
            jax.ShapeDtypeStruct((devices, tokens), F32),
        ),
        (shares, residual_in),
        flops=8 * tokens * width,
        moved=2**18,
        name="update",
    )
    squares = lax.all_to_all(
        squares.reshape(devices, 1, tokens), ("pipe", "y", "core"), 0, 0, tiled=True
    ).reshape(devices, tokens)

    return call(
        lambda *refs: norm_kernel(devices * width, *refs),
        (jax.ShapeDtypeStruct((tokens, width), BF16),) * 2,
        (updated, squares, norm_gain.reshape(1, width)),
        flops=4 * tokens * width,
        moved=2**18,
        name="norm",
    )


def solution(mesh):
    replica, pipe, tensor = mesh.devices.shape
    mesh = Mesh(
        mesh.devices.reshape(replica, pipe, tensor // 2, 2), ("replica", "pipe", "y", "core")
    )
    features = ("pipe", "y", "core")
    tensor = ("y", "core")
    in_specs = (
        P("replica", features),
        P("replica", tensor, "pipe"),
        P("replica", tensor, "pipe"),
        P("replica"),
        P("replica", features),
        P("pipe", None, tensor),
        P(features),
    )
    out_specs = (P("replica", features), P("replica", features))
    return jax.shard_map(
        on_device, mesh=mesh, in_specs=in_specs, out_specs=out_specs, check_vma=False
    )
```

```python
import math

import jax
import jax.numpy as jnp
from jax import lax
from jax.experimental import pallas as pl
from jax.experimental.pallas import tpu as pltpu
from jax.sharding import Mesh
from jax.sharding import PartitionSpec as P

HD = 128
SPAN = 32
MASKED = -1e30
FLOOR = -1e29
EPSILON = 1e-05
STATS = 16

VMEM = pl.BlockSpec(memory_space=pltpu.VMEM)
F32 = jnp.float32
BF16 = jnp.bfloat16


def call(kernel, out_shape, args, in_specs=None, scratch=(), flops=0, moved=0, name=None):
    return pl.pallas_call(
        kernel,
        out_shape=out_shape,
        in_specs=in_specs or [VMEM] * len(args),
        out_specs=jax.tree.map(lambda _: VMEM, out_shape),
        scratch_shapes=list(scratch),
        compiler_params=pltpu.CompilerParams(vmem_limit_bytes=24 * 2**20),
        cost_estimate=pl.CostEstimate(flops=flops, bytes_accessed=moved, transcendentals=0),
        name=name,
    )(*args)


def arrange_kernel(queries, out):
    heads = queries.shape[0] // 2
    rows = heads * SPAN
    blank = jnp.zeros((rows, HD), BF16)
    for request in range(out.shape[0]):
        for group in range(2):
            for of in range(2):
                out[request, pl.ds(rows * group, rows), pl.ds(HD * of, HD)] = (
                    queries[pl.ds(heads * group, heads), pl.ds(SPAN * request, SPAN), :].reshape(rows, HD)
                    if of == group
                    else blank
                )


def attend_kernel(prefix, queries, keys, values, other_keys, other_values, out):
    requests, slots, width = keys.shape
    rows = width
    slot = lax.broadcasted_iota(jnp.int32, (slots, rows), 0)
    line = lax.broadcasted_iota(jnp.int32, (STATS, rows), 0)
    lane = lax.rem(lax.broadcasted_iota(jnp.int32, (1, rows), 1), SPAN)
    core = lax.axis_index("core")
    chunk = 2 * lax.axis_index("y") + core
    offsets = (lane - chunk * slots, lane - (chunk + 1 - 2 * core) * slots)
    scale = math.log2(math.e) / math.sqrt(HD)
    for request in range(requests):
        wanted = queries[request]
        scores = []
        for key, offset in zip((keys, other_keys), offsets):
            score = lax.dot_general(
                key[request], wanted, (((1,), (1,)), ((), ())), preferred_element_type=F32
            )
            visible = slot <= prefix[:, request : request + 1] + offset
            scores.append(jnp.where(visible, score * scale, MASKED))
        peak = jnp.maximum(*[jnp.max(s, axis=0, keepdims=True) for s in scores])
        peak = jnp.maximum(peak, FLOOR).astype(BF16).astype(F32)
        weights = [jnp.exp2(s - peak) for s in scores]
        total = sum(jnp.sum(w, axis=0, keepdims=True) for w in weights)
        summed = sum(
            lax.dot_general(
                value[request], w.astype(BF16), (((0,), (0,)), ((), ())), preferred_element_type=F32
            )
            for value, w in zip((values, other_values), weights)
        )
        inverse = jnp.where(total > 0, 1.0 / total, 0.0)
        high = total.astype(BF16).astype(F32)
        stats = jnp.where(
            line == 0, peak, jnp.where(line == 1, high, jnp.where(line == 2, total - high, 0.0))
        ).astype(BF16)
        for group in range(2):
            part = slice(group * HD, (group + 1) * HD)
            out[2 * request + group, pl.ds(0, HD), :] = (summed[part, part] * inverse[:, part]).astype(BF16)
            out[2 * request + group, pl.ds(HD, STATS), :] = stats[:, part]


def combine_kernel(parts, out):
    count = parts.shape[0]
    stats = [parts[i, pl.ds(HD, STATS), :].astype(F32) for i in range(count)]
    peaks = [s[0:1] for s in stats]
    overall = peaks[0]
    for peak in peaks[1:]:
        overall = jnp.maximum(overall, peak)
    shares = [(s[1:2] + s[2:3]) * jnp.exp2(p - overall) for s, p in zip(stats, peaks)]
    inverse = 1.0 / sum(shares)
    summed = jnp.zeros((HD, HD), F32)
    for i in range(count):
        summed += parts[i, pl.ds(0, HD), :].astype(F32) * (shares[i] * inverse)
    attended = summed.T.astype(BF16)
    for i in range(count):
        out[i] = attended


def project_kernel(attended, weight, out, joined):
    for core in range(2):
        for place in range(attended.shape[1]):
            request, group = place // 2, place % 2
            for j in range(4):
                joined[
                    pl.ds(SPAN * request, SPAN), pl.ds((8 * group + 2 * j + core) * HD, HD)
                ] = attended[core, place, pl.ds(SPAN * j, SPAN), :]
    for pair in range(2):
        product = jnp.dot(
            joined[...], weight[:, pl.ds(2 * HD * pair, 2 * HD)], preferred_element_type=F32
        ).astype(BF16)
        out[2 * pair] = product[:, :HD]
        out[2 * pair + 1] = product[:, HD:]


def update_kernel(shares, residual, updated, squares):
    total = residual[...].astype(F32)
    for i in range(shares.shape[0]):
        total += shares[i].astype(F32)
    updated[...] = total
    own = jnp.sum(total * total, axis=1, keepdims=True)
    row = jnp.broadcast_to(own, total.shape).T[0:8]
    for i in range(squares.shape[0] // 8):
        squares[pl.ds(8 * i, 8), :] = row


def norm_kernel(width, updated, squares, gain, rounded, out):
    rounded[...] = updated[...].astype(BF16)
    total = jnp.sum(squares[...], axis=0, keepdims=True)
    factor = lax.rsqrt(total / width + EPSILON)
    column = jnp.broadcast_to(factor, updated.shape).T
    out[...] = (updated[...] * column * gain[...]).astype(BF16)


def on_device(queries, cache_keys, cache_values, prefix_lengths, residual_in, out_weight, norm_gain):
    chips = lax.axis_size("y")
    pipes = lax.axis_size("pipe")
    devices = 2 * chips * pipes
    tokens = queries.shape[0]
    depth, groups, width = out_weight.shape
    weight = out_weight.reshape(depth, groups * width)
    gathered = lax.all_to_all(
        jnp.broadcast_to(queries, (chips, tokens, HD)), "y", 0, 0, tiled=True
    )
    swap = [(0, 1), (1, 0)]
    other_keys = lax.ppermute(cache_keys, "core", swap)
    other_values = lax.ppermute(cache_values, "core", swap)

    arranged = call(
        arrange_kernel,
        jax.ShapeDtypeStruct((cache_keys.shape[0], 2 * HD, 2 * HD), BF16),
        (gathered,),
        flops=2**30,
        moved=2**19,
        name="arrange",
    )
    parts = call(
        attend_kernel,
        jax.ShapeDtypeStruct((chips, HD + STATS, HD), BF16),
        (prefix_lengths.reshape(1, -1), arranged, cache_keys, cache_values, other_keys, other_values),
        in_specs=[VMEM] * 6,
        flops=4 * 2 * 2 * 512 * 256 * HD,
        moved=2**21,
        name="attend",
    )
    parts = lax.all_to_all(parts, "y", 0, 0, tiled=True)
    own = call(
        combine_kernel,
        jax.ShapeDtypeStruct((chips, HD, HD), BF16),
        (parts,),
        flops=2 * 8 * HD * HD,
        moved=2**19,
        name="combine",
    )
    half = lax.all_to_all(own, "y", 0, 0, tiled=True)
    attended = lax.all_gather(half, "core")

    shares = call(
        project_kernel,
        jax.ShapeDtypeStruct((groups, tokens, width), BF16),
        (attended.reshape(2, chips, HD, HD), weight),
        scratch=[pltpu.VMEM((tokens, depth), BF16)],
        flops=2 * tokens * depth * groups * width,
        moved=3 * 2**20,
        name="project",
    )
    shares = lax.all_to_all(shares, "pipe", 0, 0, tiled=True)
    updated, squares = call(
        update_kernel,
        (
            jax.ShapeDtypeStruct((tokens, width), F32),
            jax.ShapeDtypeStruct((devices, tokens), F32),
        ),
        (shares, residual_in),
        flops=8 * tokens * width,
        moved=2**18,
        name="update",
    )
    squares = lax.all_to_all(
        squares.reshape(devices, 1, tokens), ("pipe", "y", "core"), 0, 0, tiled=True
    ).reshape(devices, tokens)

    return call(
        lambda *refs: norm_kernel(devices * width, *refs),
        (jax.ShapeDtypeStruct((tokens, width), BF16),) * 2,
        (updated, squares, norm_gain.reshape(1, width)),
        flops=4 * tokens * width,
        moved=2**18,
        name="norm",
    )


def solution(mesh):
    replica, pipe, tensor = mesh.devices.shape
    mesh = Mesh(
        mesh.devices.reshape(replica, pipe, tensor // 2, 2), ("replica", "pipe", "y", "core")
    )
    features = ("pipe", "y", "core")
    tensor = ("y", "core")
    in_specs = (
        P("replica", features),
        P("replica", tensor, "pipe"),
        P("replica", tensor, "pipe"),
        P("replica"),
        P("replica", features),
        P("pipe", None, tensor),
        P(features),
    )
    out_specs = (P("replica", features), P("replica", features))
    return jax.shard_map(
        on_device, mesh=mesh, in_specs=in_specs, out_specs=out_specs, check_vma=False
    )
```

```python
import math

import jax
import jax.numpy as jnp
from jax import lax
from jax.experimental import pallas as pl
from jax.experimental.pallas import tpu as pltpu
from jax.sharding import Mesh
from jax.sharding import PartitionSpec as P

HD = 128
SPAN = 32
MASKED = -1e30
FLOOR = -1e29
EPSILON = 1e-05
STATS = 16

VMEM = pl.BlockSpec(memory_space=pltpu.VMEM)
F32 = jnp.float32
BF16 = jnp.bfloat16


def call(kernel, out_shape, args, in_specs=None, scratch=(), flops=0, moved=0, name=None):
    return pl.pallas_call(
        kernel,
        out_shape=out_shape,
        in_specs=in_specs or [VMEM] * len(args),
        out_specs=jax.tree.map(lambda _: VMEM, out_shape),
        scratch_shapes=list(scratch),
        compiler_params=pltpu.CompilerParams(vmem_limit_bytes=24 * 2**20),
        cost_estimate=pl.CostEstimate(flops=flops, bytes_accessed=moved, transcendentals=0),
        name=name,
    )(*args)


def arrange_kernel(queries, weight, out):
    del weight
    heads = queries.shape[0] // 2
    rows = heads * SPAN
    blank = jnp.zeros((rows, HD), BF16)
    for request in range(out.shape[0]):
        for group in range(2):
            for of in range(2):
                out[request, pl.ds(rows * group, rows), pl.ds(HD * of, HD)] = (
                    queries[pl.ds(heads * group, heads), pl.ds(SPAN * request, SPAN), :].reshape(rows, HD)
                    if of == group
                    else blank
                )


def attend_kernel(prefix, queries, keys, values, far_keys, far_values, out, other_keys, other_values, sems):
    requests, slots, width = keys.shape
    rows = width
    slot = lax.broadcasted_iota(jnp.int32, (slots, rows), 0)
    line = lax.broadcasted_iota(jnp.int32, (STATS, rows), 0)
    lane = lax.rem(lax.broadcasted_iota(jnp.int32, (1, rows), 1), SPAN)
    core = lax.axis_index("core")
    chunk = 2 * lax.axis_index("y") + core
    offsets = (lane - chunk * slots, lane - (chunk + 1 - 2 * core) * slots)
    scale = math.log2(math.e) / math.sqrt(HD)
    loads = [
        [
            pltpu.make_async_copy(source.at[r], target.at[r], sems.at[i, r])
            for i, (source, target) in enumerate(((far_keys, other_keys), (far_values, other_values)))
        ]
        for r in range(requests)
    ]
    for pair in loads:
        for load in pair:
            load.start()
    for request in range(requests):
        for load in loads[request]:
            load.wait()
        wanted = queries[request]
        scores = []
        for key, offset in zip((keys, other_keys), offsets):
            score = lax.dot_general(
                key[request], wanted, (((1,), (1,)), ((), ())), preferred_element_type=F32
            )
            visible = slot <= prefix[:, request : request + 1] + offset
            scores.append(jnp.where(visible, score * scale, MASKED))
        peak = jnp.maximum(*[jnp.max(s, axis=0, keepdims=True) for s in scores])
        peak = jnp.maximum(peak, FLOOR).astype(BF16).astype(F32)
        weights = [jnp.exp2(s - peak) for s in scores]
        total = sum(jnp.sum(w, axis=0, keepdims=True) for w in weights)
        summed = sum(
            lax.dot_general(
                value[request], w.astype(BF16), (((0,), (0,)), ((), ())), preferred_element_type=F32
            )
            for value, w in zip((values, other_values), weights)
        )
        inverse = jnp.where(total > 0, 1.0 / total, 0.0)
        high = total.astype(BF16).astype(F32)
        stats = jnp.where(
            line == 0, peak, jnp.where(line == 1, high, jnp.where(line == 2, total - high, 0.0))
        ).astype(BF16)
        for group in range(2):
            part = slice(group * HD, (group + 1) * HD)
            out[2 * request + group, pl.ds(0, HD), :] = (summed[part, part] * inverse[:, part]).astype(BF16)
            out[2 * request + group, pl.ds(HD, STATS), :] = stats[:, part]


def combine_kernel(parts, out):
    count = parts.shape[0]
    stats = [parts[i, pl.ds(HD, STATS), :].astype(F32) for i in range(count)]
    peaks = [s[0:1] for s in stats]
    overall = peaks[0]
    for peak in peaks[1:]:
        overall = jnp.maximum(overall, peak)
    shares = [(s[1:2] + s[2:3]) * jnp.exp2(p - overall) for s, p in zip(stats, peaks)]
    inverse = 1.0 / sum(shares)
    summed = jnp.zeros((HD, HD), F32)
    for i in range(count):
        summed += parts[i, pl.ds(0, HD), :].astype(F32) * (shares[i] * inverse)
    attended = summed.T.astype(BF16)
    for i in range(count):
        out[i] = attended


def project_kernel(attended, weight, out, joined):
    for core in range(2):
        for place in range(attended.shape[1]):
            request, group = place // 2, place % 2
            for j in range(4):
                joined[
                    pl.ds(SPAN * request, SPAN), pl.ds((8 * group + 2 * j + core) * HD, HD)
                ] = attended[core, place, pl.ds(SPAN * j, SPAN), :]
    for pair in range(2):
        product = jnp.dot(
            joined[...], weight[:, pl.ds(2 * HD * pair, 2 * HD)], preferred_element_type=F32
        ).astype(BF16)
        out[2 * pair] = product[:, :HD]
        out[2 * pair + 1] = product[:, HD:]


def update_kernel(shares, residual, updated, squares):
    total = residual[...].astype(F32)
    for i in range(shares.shape[0]):
        total += shares[i].astype(F32)
    updated[...] = total
    own = jnp.sum(total * total, axis=1, keepdims=True)
    row = jnp.broadcast_to(own, total.shape).T[0:8]
    for i in range(squares.shape[0] // 8):
        squares[pl.ds(8 * i, 8), :] = row


def norm_kernel(width, updated, squares, gain, rounded, out):
    rounded[...] = updated[...].astype(BF16)
    total = jnp.sum(squares[...], axis=0, keepdims=True)
    factor = lax.rsqrt(total / width + EPSILON)
    column = jnp.broadcast_to(factor, updated.shape).T
    out[...] = (updated[...] * column * gain[...]).astype(BF16)


def on_device(queries, cache_keys, cache_values, prefix_lengths, residual_in, out_weight, norm_gain):
    chips = lax.axis_size("y")
    pipes = lax.axis_size("pipe")
    devices = 2 * chips * pipes
    tokens = queries.shape[0]
    depth, groups, width = out_weight.shape
    weight = out_weight.reshape(depth, groups * width)
    gathered = lax.all_to_all(
        jnp.broadcast_to(queries, (chips, tokens, HD)), "y", 0, 0, tiled=True
    )
    swap = [(0, 1), (1, 0)]
    other_keys = lax.ppermute(cache_keys, "core", swap)
    other_values = lax.ppermute(cache_values, "core", swap)

    arranged = call(
        arrange_kernel,
        jax.ShapeDtypeStruct((cache_keys.shape[0], 2 * HD, 2 * HD), BF16),
        (gathered, weight),
        in_specs=[VMEM, pl.BlockSpec(memory_space=pl.ANY)],
        flops=2**30,
        moved=2**19,
        name="arrange",
    )
    parts = call(
        attend_kernel,
        jax.ShapeDtypeStruct((chips, HD + STATS, HD), BF16),
        (prefix_lengths.reshape(1, -1), arranged, cache_keys, cache_values, other_keys, other_values),
        in_specs=[VMEM] * 4 + [pl.BlockSpec(memory_space=pltpu.HBM)] * 2,
        scratch=[
            pltpu.VMEM(cache_keys.shape, BF16),
            pltpu.VMEM(cache_values.shape, BF16),
            pltpu.SemaphoreType.DMA((2, cache_keys.shape[0])),
        ],
        flops=4 * 2 * 2 * 512 * 256 * HD,
        moved=2**21,
        name="attend",
    )
    parts = lax.all_to_all(parts, "y", 0, 0, tiled=True)
    own = call(
        combine_kernel,
        jax.ShapeDtypeStruct((chips, HD, HD), BF16),
        (parts,),
        flops=2 * 8 * HD * HD,
        moved=2**19,
        name="combine",
    )
    half = lax.all_to_all(own, "y", 0, 0, tiled=True)
    attended = lax.all_gather(half, "core")

    shares = call(
        project_kernel,
        jax.ShapeDtypeStruct((groups, tokens, width), BF16),
        (attended.reshape(2, chips, HD, HD), weight),
        scratch=[pltpu.VMEM((tokens, depth), BF16)],
        flops=2 * tokens * depth * groups * width,
        moved=3 * 2**20,
        name="project",
    )
    shares = lax.all_to_all(shares, "pipe", 0, 0, tiled=True)
    updated, squares = call(
        update_kernel,
        (
            jax.ShapeDtypeStruct((tokens, width), F32),
            jax.ShapeDtypeStruct((devices, tokens), F32),
        ),
        (shares, residual_in),
        flops=8 * tokens * width,
        moved=2**18,
        name="update",
    )
    squares = lax.all_to_all(
        squares.reshape(devices, 1, tokens), ("pipe", "y", "core"), 0, 0, tiled=True
    ).reshape(devices, tokens)

    return call(
        lambda *refs: norm_kernel(devices * width, *refs),
        (jax.ShapeDtypeStruct((tokens, width), BF16),) * 2,
        (updated, squares, norm_gain.reshape(1, width)),
        flops=4 * tokens * width,
        moved=2**18,
        name="norm",
    )


def solution(mesh):
    replica, pipe, tensor = mesh.devices.shape
    mesh = Mesh(
        mesh.devices.reshape(replica, pipe, tensor // 2, 2), ("replica", "pipe", "y", "core")
    )
    features = ("pipe", "y", "core")
    tensor = ("y", "core")
    in_specs = (
        P("replica", features),
        P("replica", tensor, "pipe"),
        P("replica", tensor, "pipe"),
        P("replica"),
        P("replica", features),
        P("pipe", None, tensor),
        P(features),
    )
    out_specs = (P("replica", features), P("replica", features))
    return jax.shard_map(
        on_device, mesh=mesh, in_specs=in_specs, out_specs=out_specs, check_vma=False
    )
```
